32 devices in a mesh: line: 4 (over y, x), plane: 8 (over z, core).
Axes of the slice: x: 2, y: 2, z: 4, core: 2. Of those that a mesh axis runs over, the one named last changes fastest.
Arguments:
- flux_x: float32 [256, 5, 8192], P('line', None, 'plane'), may hold values from -1600 to 1600
- flux_z: float32 [256, 5, 8192], P('line', None, 'plane'), may hold values from -1600 to 1600
- viscous: float32 [256, 8192], P('line', 'plane'), may hold values from 4000 to 16000
- jacobian: float32 [256, 5, 5, 8192], P('line', None, None, 'plane'), may hold values from -10 to 10
Outputs:
- delta: float32 [256, 5, 8192], P('line', None, 'plane')
The draws below stay inside these ranges and needn't reach their ends.
All inputs are finite; a program needn't handle non-finite values.
Results may differ from the reference program's by a relative error of at most 0.0003.
Values sent between devices are 32-bit elements; how exact they have to be, the bound alone decides.
A program may use at most 192 MiB of HBM per device.

```python
import math
import jax
import jax.numpy as jnp
from jax import lax

NVAR = 5
NX = 256
NZ = 8192


def block_scale(rng, dims, pieces, least, high):
    def one(dim, parts):
        heights = jax.random.uniform(jax.random.fold_in(jax.random.fold_in(rng, 6), dim), (parts,), jnp.float32, least / len(pieces), high / len(pieces))
        return jnp.repeat(jnp.exp(heights), dims[dim] // parts).reshape((-1,) + (1,) * (len(dims) - dim - 1))

    loudness = one(*pieces[0])
    for cut in pieces[1:]:
        loudness = loudness * one(*cut)
    return loudness


def bell_draw(own_key, dims, width, bound, shards=(), kind=jnp.bfloat16):
    level = block_scale(own_key, dims, shards, -0.22, 0.18) if shards else 1.0
    values = jax.random.normal(own_key, dims, jnp.float32) * width * level
    return jnp.minimum(jnp.maximum(values, -bound), bound).astype(kind)


def setup_inputs(seed: int = 0) -> dict:
    key_of = jax.random.split(jax.random.key(seed), 5)
    flux_x = bell_draw(key_of[0], (NX, NVAR, NZ), 200.0, 1600.0, ((0, 4), (2, 8)), jnp.float32)
    flux_z = bell_draw(key_of[1], (NX, NVAR, NZ), 200.0, 1600.0, ((0, 4), (2, 8)), jnp.float32)
    viscous = jnp.clip(jnp.exp(math.log(16000.0) - 1.3862944 * jax.random.uniform(key_of[2], (NX, NZ), jnp.float32) ** block_scale(key_of[2], (NX, NZ), ((0, 4), (1, 8)), -0.2, 0.2)), 4000.0, 16000.0)
    jacobian = jnp.clip(jax.random.uniform(key_of[3], (NX, NVAR, NVAR, NZ), jnp.float32, -10.0, 10.0) * block_scale(key_of[3], (NX, NVAR, NVAR, NZ), ((0, 4), (3, 8)), -0.4, 0.0), -10.0, 10.0)
    return dict(flux_x=flux_x, flux_z=flux_z, viscous=viscous, jacobian=jacobian)


courant = 10.0


def combine_blocks(matrix, operand):
    return jnp.sum(matrix[:, :, None, :] * operand[None, :, :, :], axis=1)


def solve_small(matrix, columns):
    extent = matrix.shape[0]
    for column in range(extent):
        inverse = 1.0 / matrix[column, column]
        pivot_row = matrix[column] * inverse
        column_row = columns[column] * inverse
        factor = matrix[:, column]
        matrix = matrix - factor[:, None, :] * pivot_row[None]
        columns = columns - factor[:, None, :] * column_row[None]
        matrix = matrix.at[column].set(pivot_row)
        columns = columns.at[column].set(column_row)
    return columns


def cell_blocks(viscous, jacobian):
    identity = jnp.eye(5, dtype=jnp.float32)[:, :, None]
    spread = viscous[None, None, :]
    lower_block = -spread * identity - jacobian
    center_block = (1.0 + 2.0 * spread) * identity
    upper_block = -spread * identity + jacobian
    return lower_block, center_block, upper_block


def eliminate(previous, lower_block, center_block, upper_block, source):
    extent = center_block.shape[0]
    schur = center_block - combine_blocks(lower_block, previous[:, :extent])
    moved = source - combine_blocks(lower_block, previous[:, extent:])
    return solve_small(schur, jnp.concatenate([upper_block, moved], 1))


def back_substitute(factors, extent):
    def retreat(following, factor):
        current = factor[:, extent:] - combine_blocks(factor[:, :extent], following)
        return current, current
    initial = jnp.zeros((factors.shape[1], factors.shape[2] - extent, factors.shape[3]), jnp.float32)
    _, values = lax.scan(retreat, initial, factors, reverse=True)
    return values


def reference(flux_x, flux_z, viscous, jacobian):
    pad_x = jnp.pad(flux_x, ((1, 1), (0, 0), (0, 0)))
    pad_z = jnp.pad(flux_z, ((0, 0), (0, 0), (1, 1)))
    source = -0.5 * courant * (pad_x[2:] - pad_x[:-2]) - 0.5 * courant * (pad_z[:, :, 2:] - pad_z[:, :, :-2])
    block_width = math.gcd(NZ, 2048)
    groups = NZ // block_width

    def split_lines(array):
        return jnp.moveaxis(array.reshape(array.shape[:-1] + (groups, block_width)), -2, 0)

    def solve_group(inputs):
        vis_group, jac_group, src_group = inputs

        def advance(previous, cell):
            lower_block, center_block, upper_block = cell_blocks(cell[0], cell[1])
            result = eliminate(previous, lower_block, center_block, upper_block, cell[2][:, None, :])
            return result, result
        initial = jnp.zeros((5, 6, block_width), jnp.float32)
        _, factors = lax.scan(advance, initial, (vis_group, jac_group, src_group))
        return back_substitute(factors, 5)[:, :, 0, :]

    solved = lax.map(solve_group, (split_lines(viscous), split_lines(jacobian), split_lines(source)))
    return jnp.moveaxis(solved, 0, -2).reshape(NX, 5, NZ)
```

```python
import functools
import jax
import jax.numpy as jnp
from jax import lax
from jax.experimental import pallas as pl
from jax.experimental.pallas import tpu as pltpu
from jax.sharding import PartitionSpec as P

courant = 10.0
MESH = pl.DeviceIdType.MESH
GROUPS = ((0, 4), (4, 4), (8, 3))
CHUNKS = 8
UNROLL = 2


def padded(block, axis, dim):
    count = lax.axis_size(axis)
    forward = [(i, i + 1) for i in range(count - 1)]
    backward = [(target, source) for source, target in forward]
    low = lax.ppermute(
        lax.slice_in_dim(block, block.shape[dim] - 1, None, axis=dim), axis, forward
    )
    high = lax.ppermute(lax.slice_in_dim(block, 0, 1, axis=dim), axis, backward)
    return jnp.concatenate([low, block, high], axis=dim)


def product(left, right):
    total = left[:, 0][:, None] * right[0][None]
    for k in range(1, 5):
        total = total + left[:, k][:, None] * right[k][None]
    return total


def apply(left, vector):
    total = left[:, 0] * vector[0][None]
    for k in range(1, 5):
        total = total + left[:, k] * vector[k][None]
    return total


def inverse(rows):
    a = [[rows[r, c] for c in range(5)] for r in range(5)]
    for k in range(5):
        pivot = 1.0 / a[k][k]
        for c in range(5):
            if c != k:
                a[k][c] = a[k][c] * pivot
        for r in range(5):
            if r != k:
                factor = a[r][k]
                for c in range(5):
                    if c != k:
                        a[r][c] = a[r][c] - factor * a[k][c]
                a[r][k] = -factor * pivot
        a[k][k] = pivot
    return jnp.stack([jnp.stack(row) for row in a])


def kernel(
    count, jac_hbm, vis_ref, src_ref, out_ref,
    jac, fac, basis, ends, msg, in_outer, in_mid, x_msg, in_x,
    inv_ref, free_ref, lead, jac_sem, send_sem, recv_sem,
):
    cells = vis_ref.shape[0]
    tile = vis_ref.shape[1:]
    me = lax.axis_index("line")
    half = count // 2
    step = cells // CHUNKS

    def fetch(chunk):
        part = pl.ds(chunk * step, step)
        return pltpu.make_async_copy(jac_hbm.at[part], jac.at[part], jac_sem.at[chunk])

    for chunk in range(CHUNKS):
        fetch(chunk).start()

    barrier = pltpu.get_barrier_semaphore()

    @pl.when(me > 0)
    def _():
        pl.semaphore_signal(barrier, inc=1, device_id={"line": me - 1}, device_id_type=MESH)

    @pl.when(me < count - 1)
    def _():
        pl.semaphore_signal(barrier, inc=1, device_id={"line": me + 1}, device_id_type=MESH)

    def factor_cell(i):
        v = vis_ref[i]
        a = [[jac[i, r, c, :].reshape(tile) for c in range(5)] for r in range(5)]
        for k in range(5):
            a[k][k] = a[k][k] - v
        for k in range(5):
            pivot = 1.0 / a[k][k]
            for r in range(k + 1, 5):
                a[r][k] = a[r][k] * pivot
                for c in range(k + 1, 5):
                    a[r][c] = a[r][c] - a[r][k] * a[k][c]
            a[k][k] = -pivot
            for c in range(k + 1, 5):
                a[k][c] = a[k][c] * pivot
        for r in range(5):
            for c in range(5):
                fac[i, r * 5 + c] = a[r][c]

    def factor_chunk(chunk, _):
        fetch(chunk).wait()

        def body(j, _):
            for u in range(UNROLL):
                factor_cell(chunk * step + j * UNROLL + u)
            return 0

        return lax.fori_loop(0, step // UNROLL, body, 0)

    lax.fori_loop(0, CHUNKS, factor_chunk, 0)

    def march(first, width):
        has_source = first + width == 11

        def start(low):
            return [
                jnp.stack([
                    jnp.full(tile, 1.0 if first + c == low + r else 0.0, jnp.float32)
                    for c in range(width)
                ])
                for r in range(5)
            ]

        def body(i, state):
            x, d = list(state[:5]), list(state[5:])
            twice = (vis_ref[i] * 2.0)[None]
            w = []
            for r in range(5):
                x[r] = x[r] + d[r]
                basis[i, r, pl.ds(first, width)] = x[r]
                w.append(x[r] + twice * d[r])
            if has_source:
                w = [
                    jnp.concatenate([w[r][: width - 1], w[r][width - 1:] - src_ref[i, r][None]], 0)
                    for r in range(5)
                ]
            f = [[fac[i, r * 5 + c][None] for c in range(5)] for r in range(5)]
            for r in range(1, 5):
                for c in range(r):
                    w[r] = w[r] - f[r][c] * w[c]
            for r in range(4, -1, -1):
                w[r] = w[r] * f[r][r]
                for c in range(r + 1, 5):
                    w[r] = w[r] - f[r][c] * w[c]
            d = [w[r] - d[r] for r in range(5)]
            return (*x, *d)

        state = lax.fori_loop(0, cells, body, (*start(0), *start(5)))
        for r in range(10):
            ends[r, pl.ds(first, width)] = state[r]

    for first, width in GROUPS:
        march(first, width)

    pl.semaphore_wait(barrier, (me > 0).astype(jnp.int32) + (me < count - 1).astype(jnp.int32))

    t11, t12 = lambda: ends[0:5, 0:5], lambda: ends[0:5, 5:10]
    t21, t22 = lambda: ends[5:10, 0:5], lambda: ends[5:10, 5:10]
    t1, t2 = lambda: ends[0:5, 10], lambda: ends[5:10, 10]

    def send_relation(target, place, slot):
        return pltpu.make_async_remote_copy(
            src_ref=msg, dst_ref=place, send_sem=send_sem.at[0], recv_sem=recv_sem.at[slot],
            device_id={"line": target}, device_id_type=MESH,
        )

    def send_x(target):
        return pltpu.make_async_remote_copy(
            src_ref=x_msg, dst_ref=in_x, send_sem=send_sem.at[1], recv_sem=recv_sem.at[2],
            device_id={"line": target}, device_id_type=MESH,
        )

    @pl.when((me > 0) & (me < count - 1))
    def _():
        send_relation(me, in_outer, 0).wait_recv()

    @pl.when(me < half)
    def _():
        @pl.when(me == 0)
        def _():
            lead[0:5, 0:5] = t12()
            lead[5:10, 0:5] = t22()
            lead[0:5, 5] = t1()
            lead[5:10, 5] = t2()

        @pl.when(me > 0)
        def _():
            q = in_outer[:, 0:6]
            lead[0:5, 0:6] = product(t12(), q)
            lead[5:10, 0:6] = product(t22(), q)
            lead[:, 0:5] = lead[:, 0:5] + ends[:, 0:5]
            lead[:, 5] = lead[:, 5] + ends[:, 10]

        inv = inverse(lead[0:5, 0:5])
        inv_ref[...] = inv
        q = product(lead[5:10, 0:5], inv)
        msg[:, 0:5] = q
        msg[:, 5] = lead[5:10, 5] - apply(q, lead[0:5, 5])

    @pl.when(me >= half)
    def _():
        @pl.when(me == count - 1)
        def _():
            free_ref[...] = t12() + t22()
            lead[0:5, 0:5] = -(t11() + t21())
            lead[0:5, 5] = -(t1() + t2())

        @pl.when(me < count - 1)
        def _():
            q = in_outer[:, 0:5]
            free_ref[...] = t22() - product(q, t12())
            lead[0:5, 0:5] = product(q, t11()) - t21()
            lead[0:5, 5] = apply(q, t1()) + in_outer[:, 5] - t2()

        msg[...] = product(inverse(free_ref[...]), lead[0:5, 0:6])

    @pl.when(me < half - 1)
    def _():
        send_relation(me + 1, in_outer, 0).start()

    @pl.when(me == half - 1)
    def _():
        send_relation(me + 1, in_mid, 1).start()

    @pl.when(me == half)
    def _():
        send_relation(me - 1, in_mid, 1).start()

    @pl.when(me > half)
    def _():
        send_relation(me - 1, in_outer, 0).start()

    middle = (me == half - 1) | (me == half)

    @pl.when(middle)
    def _():
        send_relation(me, in_mid, 1).wait_recv()
        gap = msg[...] - in_mid[...]
        in_x[...] = -apply(inverse(gap[:, 0:5]), gap[:, 5])

    @pl.when(jnp.logical_not(middle))
    def _():
        send_x(me).wait_recv()

    @pl.when(me < half)
    def _():
        found = apply(inv_ref[...], in_x[...] - lead[0:5, 5])

        @pl.when(me == 0)
        def _():
            lead[0:5, 6] = jnp.zeros((5,) + tile, jnp.float32)
            lead[5:10, 6] = found

        @pl.when(me > 0)
        def _():
            x_msg[...] = found
            send_x(me - 1).start()
            lead[0:5, 6] = found
            lead[5:10, 6] = apply(in_outer[:, 0:5], found) + in_outer[:, 5]

    @pl.when(me >= half)
    def _():
        x = in_x[...]
        d = apply(msg[:, 0:5], x) + msg[:, 5]
        lead[0:5, 6] = x
        lead[5:10, 6] = d

        @pl.when(me < count - 1)
        def _():
            x_msg[...] = apply(t11(), x) + apply(t12(), d) + t1()
            send_x(me + 1).start()

    z = [lead[k, 6] for k in range(10)]

    def finish(i, _):
        for r in range(5):
            terms = [basis[i, r, k] * z[k] for k in range(10)] + [basis[i, r, 10]]
            while len(terms) > 1:
                terms = [sum(terms[k + 1:k + 2], terms[k]) for k in range(0, len(terms), 2)]
            out_ref[i, r] = terms[0]
        return 0

    lax.fori_loop(0, cells, finish, 0)

    send_relation(me, in_outer, 0).wait_send()

    @pl.when((me > 0) & (me < count - 1))
    def _():
        send_x(me).wait_send()


def per_device(flux_x, flux_z, viscous, jacobian):
    stream = padded(flux_x, "line", 0)
    across = padded(flux_z, "plane", 2)
    source = -0.5 * courant * (stream[2:] - stream[:-2]) - 0.5 * courant * (
        across[:, :, 2:] - across[:, :, :-2]
    )
    cells, lines = viscous.shape
    tile = (lines // 128, 128)
    count = lax.axis_size("line")
    f32 = jnp.float32
    vmem = pl.BlockSpec(memory_space=pltpu.VMEM)
    delta = pl.pallas_call(
        functools.partial(kernel, count),
        out_shape=jax.ShapeDtypeStruct((cells, 5) + tile, f32),
        in_specs=[pl.BlockSpec(memory_space=pl.ANY), vmem, vmem],
        out_specs=vmem,
        scratch_shapes=[
            pltpu.VMEM((cells, 5, 5, lines), f32),
            pltpu.VMEM((cells, 25) + tile, f32),
            pltpu.VMEM((cells, 5, 11) + tile, f32),
            pltpu.VMEM((10, 11) + tile, f32),
            pltpu.VMEM((5, 6) + tile, f32),
            pltpu.VMEM((5, 6) + tile, f32),
            pltpu.VMEM((5, 6) + tile, f32),
            pltpu.VMEM((5,) + tile, f32),
            pltpu.VMEM((5,) + tile, f32),
            pltpu.VMEM((5, 5) + tile, f32),
            pltpu.VMEM((5, 5) + tile, f32),
            pltpu.VMEM((10, 7) + tile, f32),
            pltpu.SemaphoreType.DMA((CHUNKS,)),
            pltpu.SemaphoreType.DMA((2,)),
            pltpu.SemaphoreType.DMA((3,)),
        ],
        compiler_params=pltpu.CompilerParams(
            collective_id=0, has_side_effects=True, vmem_limit_bytes=56 * 1024 * 1024
        ),
    )(jacobian, viscous.reshape((cells,) + tile), source.reshape((cells, 5) + tile))
    return delta.reshape(cells, 5, lines)


def solution(mesh):
    placed = (
        P("line", None, "plane"),
        P("line", None, "plane"),
        P("line", "plane"),
        P("line", None, None, "plane"),
    )
    return jax.shard_map(
        per_device, mesh=mesh, in_specs=placed, out_specs=P("line", None, "plane"), check_vma=False
    )
```

```python
import functools
import jax
import jax.numpy as jnp
from jax import lax
from jax.experimental import pallas as pl
from jax.experimental.pallas import tpu as pltpu
from jax.sharding import PartitionSpec as P

courant = 10.0
MESH = pl.DeviceIdType.MESH
GROUPS = ((0, 4), (4, 4), (8, 3))


def product(left, right):
    total = left[:, 0][:, None] * right[0][None]
    for k in range(1, 5):
        total = total + left[:, k][:, None] * right[k][None]
    return total


def apply(left, vector):
    total = left[:, 0] * vector[0][None]
    for k in range(1, 5):
        total = total + left[:, k] * vector[k][None]
    return total


def inverse(rows):
    a = [[rows[r, c] for c in range(5)] for r in range(5)]
    for k in range(5):
        pivot = 1.0 / a[k][k]
        for c in range(5):
            if c != k:
                a[k][c] = a[k][c] * pivot
        for r in range(5):
            if r != k:
                factor = a[r][k]
                for c in range(5):
                    if c != k:
                        a[r][c] = a[r][c] - factor * a[k][c]
                a[r][k] = -factor * pivot
        a[k][k] = pivot
    return jnp.stack([jnp.stack(row) for row in a])


def kernel(
    count, planes, flux_x_hbm, flux_z_hbm, vis_hbm, jac_hbm, out_ref,
    flux_x, flux_z, vis, jac, x_low, x_high, z_low, z_high, across, twice, src,
    fac, basis, ends, msg, in_outer, in_mid, x_msg, in_x, inv_ref, free_ref, lead,
    local_sem, jac_sem, halo_send, halo_recv, send_sem, recv_sem,
):
    blocks, rows, lines = vis.shape
    cells = blocks * rows
    tile = (lines // 128, 128)
    me, plane = lax.axis_index("line"), lax.axis_index("plane")
    half = count // 2

    def fetch(block):
        return pltpu.make_async_copy(jac_hbm.at[:, :, block], jac.at[:, :, block], jac_sem.at[block])

    fetch_vis = pltpu.make_async_copy(vis_hbm, vis, local_sem.at[0])
    fetch_x = pltpu.make_async_copy(flux_x_hbm, flux_x, local_sem.at[1])
    fetch_z = pltpu.make_async_copy(flux_z_hbm, flux_z, local_sem.at[2])

    fetch_vis.start()
    for block in range(blocks):
        fetch(block).start()
    fetch_x.start()
    fetch_z.start()

    def halo(slot, source, target, where):
        return pltpu.make_async_remote_copy(
            src_ref=source, dst_ref=target, send_sem=halo_send.at[slot],
            recv_sem=halo_recv.at[slot], device_id=where, device_id_type=MESH,
        )

    halos = (
        (me < count - 1, me > 0, x_low, halo(0, flux_x_hbm.at[:, blocks - 1], x_low, {"line": me + 1})),
        (me > 0, me < count - 1, x_high, halo(1, flux_x_hbm.at[:, 0], x_high, {"line": me - 1})),
        (plane < planes - 1, plane > 0, z_low,
         halo(2, flux_z_hbm.at[:, :, :, pl.ds(lines - 128, 128)], z_low, {"plane": plane + 1})),
        (plane > 0, plane < planes - 1, z_high,
         halo(3, flux_z_hbm.at[:, :, :, pl.ds(0, 128)], z_high, {"plane": plane - 1})),
    )
    barrier = pltpu.get_barrier_semaphore()
    for sends, receives, buffer, copy in halos:

        @pl.when(sends)
        def _():
            pl.semaphore_signal(barrier, inc=1, device_id=copy.device_id, device_id_type=MESH)

        @pl.when(jnp.logical_not(receives))
        def _():
            buffer[...] = jnp.zeros_like(buffer)

    pl.semaphore_wait(barrier, sum(sends.astype(jnp.int32) for sends, _, _, _ in halos))
    for sends, receives, buffer, copy in halos:

        @pl.when(sends)
        def _():
            copy.start()

    fetch_vis.wait()

    def factor_block(block, _):
        fetch(block).wait()
        for u in range(rows):
            i = block * rows + u
            v = vis[block, u, :].reshape(tile)
            twice[i] = v * 2.0
            a = [[jac[r, c, block, u, :].reshape(tile) for c in range(5)] for r in range(5)]
            for k in range(5):
                a[k][k] = a[k][k] - v
            for k in range(5):
                pivot = 1.0 / a[k][k]
                for r in range(k + 1, 5):
                    a[r][k] = a[r][k] * pivot
                    for c in range(k + 1, 5):
                        a[r][c] = a[r][c] - a[r][k] * a[k][c]
                a[k][k] = -pivot
                for c in range(k + 1, 5):
                    a[k][c] = a[k][c] * pivot
            for r in range(5):
                for c in range(5):
                    fac[i, r * 5 + c] = a[r][c]
        return 0

    lax.fori_loop(0, blocks, factor_block, 0)

    def make_source():
        fetch_x.wait()
        fetch_z.wait()
        for sends, receives, buffer, copy in halos:

            @pl.when(receives)
            def _():
                copy.wait_recv()

        lane = lax.broadcasted_iota(jnp.int32, (rows, 128), 1)

        def body(block, before):
            now = []
            for r in range(5):
                middle = flux_z[r, block]
                up = pltpu.roll(middle, lines - 1, 1)
                down = pltpu.roll(middle, 1, 1)
                first = jnp.where(lane == 0, pltpu.roll(z_low[r, block], 1, 1), down[:, :128])
                last = jnp.where(lane == 127, pltpu.roll(z_high[r, block], 127, 1), up[:, lines - 128:])
                up = jnp.concatenate([up[:, : lines - 128], last], 1)
                down = jnp.concatenate([first, down[:, 128:]], 1)
                across[r] = up - down
                here = [flux_x[r, block, u, :].reshape(tile) for u in range(rows)]
                following = flux_x[r, jnp.minimum(block + 1, blocks - 1), 0, :].reshape(tile)
                following = jnp.where(block == blocks - 1, x_high[r, 0, :].reshape(tile), following)
                stream = [before[r]] + here + [following]
                now.append(here[-1])
                for u in range(rows):
                    src[block * rows + u, r] = (-0.5 * courant) * (stream[u + 2] - stream[u]) + (
                        -0.5 * courant
                    ) * across[r, u, :].reshape(tile)
            return tuple(now)

        lax.fori_loop(0, blocks, body, tuple(x_low[r, rows - 1, :].reshape(tile) for r in range(5)))

    def march(first, width):
        has_source = first + width == 11

        def start(low):
            return [
                jnp.stack([
                    jnp.full(tile, 1.0 if first + c == low + r else 0.0, jnp.float32)
                    for c in range(width)
                ])
                for r in range(5)
            ]

        def body(i, state):
            x, d = list(state[:5]), list(state[5:])
            two = twice[i][None]
            w = []
            for r in range(5):
                x[r] = x[r] + d[r]
                basis[i, r, pl.ds(first, width)] = x[r]
                w.append(x[r] + two * d[r])
            if has_source:
                w = [
                    jnp.concatenate([w[r][: width - 1], w[r][width - 1:] - src[i, r][None]], 0)
                    for r in range(5)
                ]
            f = [[fac[i, r * 5 + c][None] for c in range(5)] for r in range(5)]
            for r in range(1, 5):
                for c in range(r):
                    w[r] = w[r] - f[r][c] * w[c]
            for r in range(4, -1, -1):
                w[r] = w[r] * f[r][r]
                for c in range(r + 1, 5):
                    w[r] = w[r] - f[r][c] * w[c]
            d = [w[r] - d[r] for r in range(5)]
            return (*x, *d)

        state = lax.fori_loop(0, cells, body, (*start(0), *start(5)))
        for r in range(10):
            ends[r, pl.ds(first, width)] = state[r]

    for first, width in GROUPS:
        if first + width == 11:
            make_source()
        march(first, width)

    t11, t12 = lambda: ends[0:5, 0:5], lambda: ends[0:5, 5:10]
    t21, t22 = lambda: ends[5:10, 0:5], lambda: ends[5:10, 5:10]
    t1, t2 = lambda: ends[0:5, 10], lambda: ends[5:10, 10]

    def send_relation(target, place, slot):
        return pltpu.make_async_remote_copy(
            src_ref=msg, dst_ref=place, send_sem=send_sem.at[0], recv_sem=recv_sem.at[slot],
            device_id={"line": target}, device_id_type=MESH,
        )

    def send_x(target):
        return pltpu.make_async_remote_copy(
            src_ref=x_msg, dst_ref=in_x, send_sem=send_sem.at[1], recv_sem=recv_sem.at[2],
            device_id={"line": target}, device_id_type=MESH,
        )

    @pl.when((me > 0) & (me < count - 1))
    def _():
        send_relation(me, in_outer, 0).wait_recv()

    @pl.when(me < half)
    def _():
        @pl.when(me == 0)
        def _():
            lead[0:5, 0:5] = t12()
            lead[5:10, 0:5] = t22()
            lead[0:5, 5] = t1()
            lead[5:10, 5] = t2()

        @pl.when(me > 0)
        def _():
            q = in_outer[:, 0:6]
            lead[0:5, 0:6] = product(t12(), q)
            lead[5:10, 0:6] = product(t22(), q)
            lead[:, 0:5] = lead[:, 0:5] + ends[:, 0:5]
            lead[:, 5] = lead[:, 5] + ends[:, 10]

        inv = inverse(lead[0:5, 0:5])
        inv_ref[...] = inv
        q = product(lead[5:10, 0:5], inv)
        msg[:, 0:5] = q
        msg[:, 5] = lead[5:10, 5] - apply(q, lead[0:5, 5])

    @pl.when(me >= half)
    def _():
        @pl.when(me == count - 1)
        def _():
            free_ref[...] = t12() + t22()
            lead[0:5, 0:5] = -(t11() + t21())
            lead[0:5, 5] = -(t1() + t2())

        @pl.when(me < count - 1)
        def _():
            q = in_outer[:, 0:5]
            free_ref[...] = t22() - product(q, t12())
            lead[0:5, 0:5] = product(q, t11()) - t21()
            lead[0:5, 5] = apply(q, t1()) + in_outer[:, 5] - t2()

        msg[...] = product(inverse(free_ref[...]), lead[0:5, 0:6])

    @pl.when(me < half - 1)
    def _():
        send_relation(me + 1, in_outer, 0).start()

    @pl.when(me == half - 1)
    def _():
        send_relation(me + 1, in_mid, 1).start()

    @pl.when(me == half)
    def _():
        send_relation(me - 1, in_mid, 1).start()

    @pl.when(me > half)
    def _():
        send_relation(me - 1, in_outer, 0).start()

    middle = (me == half - 1) | (me == half)

    @pl.when(middle)
    def _():
        send_relation(me, in_mid, 1).wait_recv()
        gap = msg[...] - in_mid[...]
        in_x[...] = -apply(inverse(gap[:, 0:5]), gap[:, 5])

    @pl.when(jnp.logical_not(middle))
    def _():
        send_x(me).wait_recv()

    @pl.when(me < half)
    def _():
        found = apply(inv_ref[...], in_x[...] - lead[0:5, 5])

        @pl.when(me == 0)
        def _():
            lead[0:5, 6] = jnp.zeros((5,) + tile, jnp.float32)
            lead[5:10, 6] = found

        @pl.when(me > 0)
        def _():
            x_msg[...] = found
            send_x(me - 1).start()
            lead[0:5, 6] = found
            lead[5:10, 6] = apply(in_outer[:, 0:5], found) + in_outer[:, 5]

    @pl.when(me >= half)
    def _():
        x = in_x[...]
        d = apply(msg[:, 0:5], x) + msg[:, 5]
        lead[0:5, 6] = x
        lead[5:10, 6] = d

        @pl.when(me < count - 1)
        def _():
            x_msg[...] = apply(t11(), x) + apply(t12(), d) + t1()
            send_x(me + 1).start()

    z = [lead[k, 6] for k in range(10)]

    def finish(block, _):
        for u in range(rows):
            i = block * rows + u
            for r in range(5):
                terms = [basis[i, r, k] * z[k] for k in range(10)] + [basis[i, r, 10]]
                while len(terms) > 1:
                    terms = [sum(terms[k + 1:k + 2], terms[k]) for k in range(0, len(terms), 2)]
                out_ref[r, block, u, :] = terms[0].reshape(lines)
        return 0

    lax.fori_loop(0, blocks, finish, 0)

    for sends, receives, buffer, copy in halos:

        @pl.when(sends)
        def _():
            copy.wait_send()

    send_relation(me, in_outer, 0).wait_send()

    @pl.when((me > 0) & (me < count - 1))
    def _():
        send_x(me).wait_send()


def per_device(flux_x, flux_z, viscous, jacobian):
    cells, lines = viscous.shape
    rows = 8
    blocks = cells // rows
    tile = (lines // 128, 128)
    f32 = jnp.float32
    line_cells = (blocks, rows, lines)
    delta = pl.pallas_call(
        functools.partial(kernel, lax.axis_size("line"), lax.axis_size("plane")),
        out_shape=jax.ShapeDtypeStruct((5,) + line_cells, f32),
        in_specs=[pl.BlockSpec(memory_space=pl.ANY)] * 4,
        out_specs=pl.BlockSpec(memory_space=pltpu.VMEM),
        scratch_shapes=[
            pltpu.VMEM((5,) + line_cells, f32),
            pltpu.VMEM((5,) + line_cells, f32),
            pltpu.VMEM(line_cells, f32),
            pltpu.VMEM((5, 5) + line_cells, f32),
            pltpu.VMEM((5, rows, lines), f32),
            pltpu.VMEM((5, rows, lines), f32),
            pltpu.VMEM((5, blocks, rows, 128), f32),
            pltpu.VMEM((5, blocks, rows, 128), f32),
            pltpu.VMEM((5, rows, lines), f32),
            pltpu.VMEM((cells,) + tile, f32),
            pltpu.VMEM((cells, 5) + tile, f32),
            pltpu.VMEM((cells, 25) + tile, f32),
            pltpu.VMEM((cells, 5, 11) + tile, f32),
            pltpu.VMEM((10, 11) + tile, f32),
            pltpu.VMEM((5, 6) + tile, f32),
            pltpu.VMEM((5, 6) + tile, f32),
            pltpu.VMEM((5, 6) + tile, f32),
            pltpu.VMEM((5,) + tile, f32),
            pltpu.VMEM((5,) + tile, f32),
            pltpu.VMEM((5, 5) + tile, f32),
            pltpu.VMEM((5, 5) + tile, f32),
            pltpu.VMEM((10, 7) + tile, f32),
            pltpu.SemaphoreType.DMA((3,)),
            pltpu.SemaphoreType.DMA((blocks,)),
            pltpu.SemaphoreType.DMA((4,)),
            pltpu.SemaphoreType.DMA((4,)),
            pltpu.SemaphoreType.DMA((2,)),
            pltpu.SemaphoreType.DMA((3,)),
        ],
        compiler_params=pltpu.CompilerParams(
            collective_id=0, has_side_effects=True, vmem_limit_bytes=56 * 1024 * 1024
        ),
    )(
        flux_x.transpose(1, 0, 2).reshape((5,) + line_cells),
        flux_z.transpose(1, 0, 2).reshape((5,) + line_cells),
        viscous.reshape(line_cells),
        jacobian.transpose(1, 2, 0, 3).reshape((5, 5) + line_cells),
    )
    return delta.reshape(5, cells, lines).transpose(1, 0, 2)


def solution(mesh):
    placed = (
        P("line", None, "plane"),
        P("line", None, "plane"),
        P("line", "plane"),
        P("line", None, None, "plane"),
    )
    return jax.shard_map(
        per_device, mesh=mesh, in_specs=placed, out_specs=P("line", None, "plane"), check_vma=False
    )
```

```python
import functools
import jax
import jax.numpy as jnp
from jax import lax
from jax.experimental import pallas as pl
from jax.experimental.pallas import tpu as pltpu
from jax.sharding import PartitionSpec as P

courant = 10.0
MESH = pl.DeviceIdType.MESH
GROUPS = ((0, 4), (4, 4), (8, 3))


def product(left, right):
    total = left[:, 0][:, None] * right[0][None]
    for k in range(1, 5):
        total = total + left[:, k][:, None] * right[k][None]
    return total


def apply(left, vector):
    total = left[:, 0] * vector[0][None]
    for k in range(1, 5):
        total = total + left[:, k] * vector[k][None]
    return total


def inverse(rows):
    a = [[rows[r, c] for c in range(5)] for r in range(5)]
    for k in range(5):
        pivot = 1.0 / a[k][k]
        for c in range(5):
            if c != k:
                a[k][c] = a[k][c] * pivot
        for r in range(5):
            if r != k:
                factor = a[r][k]
                for c in range(5):
                    if c != k:
                        a[r][c] = a[r][c] - factor * a[k][c]
                a[r][k] = -factor * pivot
        a[k][k] = pivot
    return jnp.stack([jnp.stack(row) for row in a])


def kernel(
    count, planes, flux_x_hbm, flux_z_hbm, vis_hbm, jac_hbm, out_ref,
    flux_x, flux_z, vis, jac, x_low, x_high, z_low, z_high, across, twice, src,
    fac, basis, ends, msg, in_outer, in_mid, x_msg, in_x, inv_ref, free_ref, lead,
    local_sem, jac_sem, halo_send, halo_recv, send_sem, recv_sem,
):
    blocks, rows, lines = vis.shape
    cells = blocks * rows
    tile = (lines // 128, 128)
    me, plane = lax.axis_index("line"), lax.axis_index("plane")
    half = count // 2

    def fetch(block):
        return pltpu.make_async_copy(jac_hbm.at[:, :, block], jac.at[:, :, block], jac_sem.at[block])

    fetch_vis = pltpu.make_async_copy(vis_hbm, vis, local_sem.at[0])
    fetch_x = pltpu.make_async_copy(flux_x_hbm, flux_x, local_sem.at[1])
    fetch_z = pltpu.make_async_copy(flux_z_hbm, flux_z, local_sem.at[2])

    fetch_vis.start()
    for block in range(blocks):
        fetch(block).start()
    fetch_x.start()
    fetch_z.start()

    def halo(slot, source, target, where):
        return pltpu.make_async_remote_copy(
            src_ref=source, dst_ref=target, send_sem=halo_send.at[slot],
            recv_sem=halo_recv.at[slot], device_id=where, device_id_type=MESH,
        )

    halos = (
        (me < count - 1, me > 0, x_low, halo(0, flux_x_hbm.at[:, blocks - 1], x_low, {"line": me + 1})),
        (me > 0, me < count - 1, x_high, halo(1, flux_x_hbm.at[:, 0], x_high, {"line": me - 1})),
        (plane < planes - 1, plane > 0, z_low,
         halo(2, flux_z_hbm.at[:, :, :, pl.ds(lines - 128, 128)], z_low, {"plane": plane + 1})),
        (plane > 0, plane < planes - 1, z_high,
         halo(3, flux_z_hbm.at[:, :, :, pl.ds(0, 128)], z_high, {"plane": plane - 1})),
    )
    barrier = pltpu.get_barrier_semaphore()
    for sends, receives, buffer, copy in halos:

        @pl.when(sends)
        def _():
            pl.semaphore_signal(barrier, inc=1, device_id=copy.device_id, device_id_type=MESH)

        @pl.when(jnp.logical_not(receives))
        def _():
            buffer[...] = jnp.zeros_like(buffer)

    pl.semaphore_wait(barrier, sum(sends.astype(jnp.int32) for sends, _, _, _ in halos))
    for sends, receives, buffer, copy in halos:

        @pl.when(sends)
        def _():
            copy.start()

    fetch_vis.wait()

    def factor_block(block, _):
        fetch(block).wait()
        for u in range(rows):
            i = block * rows + u
            v = vis[block, u, :].reshape(tile)
            twice[i] = v * 2.0
            a = [[jac[r, c, block, u, :].reshape(tile) for c in range(5)] for r in range(5)]
            for k in range(5):
                a[k][k] = a[k][k] - v
            for k in range(5):
                pivot = 1.0 / a[k][k]
                for r in range(k + 1, 5):
                    a[r][k] = a[r][k] * pivot
                    for c in range(k + 1, 5):
                        a[r][c] = a[r][c] - a[r][k] * a[k][c]
                a[k][k] = -pivot
                for c in range(k + 1, 5):
                    a[k][c] = a[k][c] * pivot
            for r in range(5):
                for c in range(5):
                    fac[i, r * 5 + c] = a[r][c]
        return 0

    lax.fori_loop(0, blocks, factor_block, 0)

    def make_source():
        fetch_x.wait()
        fetch_z.wait()
        for sends, receives, buffer, copy in halos:

            @pl.when(receives)
            def _():
                copy.wait_recv()

        lane = lax.broadcasted_iota(jnp.int32, (rows, 128), 1)

        def body(block, before):
            now = []
            for r in range(5):
                middle = flux_z[r, block]
                up = pltpu.roll(middle, lines - 1, 1)
                down = pltpu.roll(middle, 1, 1)
                first = jnp.where(lane == 0, pltpu.roll(z_low[r, block], 1, 1), down[:, :128])
                last = jnp.where(lane == 127, pltpu.roll(z_high[r, block], 127, 1), up[:, lines - 128:])
                up = jnp.concatenate([up[:, : lines - 128], last], 1)
                down = jnp.concatenate([first, down[:, 128:]], 1)
                across[r] = up - down
                here = [flux_x[r, block, u, :].reshape(tile) for u in range(rows)]
                following = flux_x[r, jnp.minimum(block + 1, blocks - 1), 0, :].reshape(tile)
                following = jnp.where(block == blocks - 1, x_high[r, 0, :].reshape(tile), following)
                stream = [before[r]] + here + [following]
                now.append(here[-1])
                for u in range(rows):
                    src[block * rows + u, r] = (-0.5 * courant) * (stream[u + 2] - stream[u]) + (
                        -0.5 * courant
                    ) * across[r, u, :].reshape(tile)
            return tuple(now)

        lax.fori_loop(0, blocks, body, tuple(x_low[r, rows - 1, :].reshape(tile) for r in range(5)))

    def march(first, width):
        has_source = first + width == 11

        def start(low):
            return [
                jnp.stack([
                    jnp.full(tile, 1.0 if first + c == low + r else 0.0, jnp.float32)
                    for c in range(width)
                ])
                for r in range(5)
            ]

        def body(i, state):
            x, d = list(state[:5]), list(state[5:])
            two = twice[i][None]
            w = []
            for r in range(5):
                x[r] = x[r] + d[r]
                basis[i, r, pl.ds(first, width)] = x[r]
                w.append(x[r] + two * d[r])
            if has_source:
                w = [
                    jnp.concatenate([w[r][: width - 1], w[r][width - 1:] - src[i, r][None]], 0)
                    for r in range(5)
                ]
            f = [[fac[i, r * 5 + c][None] for c in range(5)] for r in range(5)]
            for r in range(1, 5):
                for c in range(r):
                    w[r] = w[r] - f[r][c] * w[c]
            for r in range(4, -1, -1):
                w[r] = w[r] * f[r][r]
                for c in range(r + 1, 5):
                    w[r] = w[r] - f[r][c] * w[c]
            d = [w[r] - d[r] for r in range(5)]
            return (*x, *d)

        state = lax.fori_loop(0, cells, body, (*start(0), *start(5)), unroll=2)
        for r in range(10):
            ends[r, pl.ds(first, width)] = state[r]

    for first, width in GROUPS:
        if first + width == 11:
            make_source()
        march(first, width)

    t11, t12 = lambda: ends[0:5, 0:5], lambda: ends[0:5, 5:10]
    t21, t22 = lambda: ends[5:10, 0:5], lambda: ends[5:10, 5:10]
    t1, t2 = lambda: ends[0:5, 10], lambda: ends[5:10, 10]

    def send_relation(target, place, slot):
        return pltpu.make_async_remote_copy(
            src_ref=msg, dst_ref=place, send_sem=send_sem.at[0], recv_sem=recv_sem.at[slot],
            device_id={"line": target}, device_id_type=MESH,
        )

    def send_x(target):
        return pltpu.make_async_remote_copy(
            src_ref=x_msg, dst_ref=in_x, send_sem=send_sem.at[1], recv_sem=recv_sem.at[2],
            device_id={"line": target}, device_id_type=MESH,
        )

    @pl.when((me > 0) & (me < count - 1))
    def _():
        send_relation(me, in_outer, 0).wait_recv()

    @pl.when(me < half)
    def _():
        @pl.when(me == 0)
        def _():
            lead[0:5, 0:5] = t12()
            lead[5:10, 0:5] = t22()
            lead[0:5, 5] = t1()
            lead[5:10, 5] = t2()

        @pl.when(me > 0)
        def _():
            q = in_outer[:, 0:6]
            lead[0:5, 0:6] = product(t12(), q)
            lead[5:10, 0:6] = product(t22(), q)
            lead[:, 0:5] = lead[:, 0:5] + ends[:, 0:5]
            lead[:, 5] = lead[:, 5] + ends[:, 10]

        inv = inverse(lead[0:5, 0:5])
        inv_ref[...] = inv
        q = product(lead[5:10, 0:5], inv)
        msg[:, 0:5] = q
        msg[:, 5] = lead[5:10, 5] - apply(q, lead[0:5, 5])

    @pl.when(me >= half)
    def _():
        @pl.when(me == count - 1)
        def _():
            free_ref[...] = t12() + t22()
            lead[0:5, 0:5] = -(t11() + t21())
            lead[0:5, 5] = -(t1() + t2())

        @pl.when(me < count - 1)
        def _():
            q = in_outer[:, 0:5]
            free_ref[...] = t22() - product(q, t12())
            lead[0:5, 0:5] = product(q, t11()) - t21()
            lead[0:5, 5] = apply(q, t1()) + in_outer[:, 5] - t2()

        msg[...] = product(inverse(free_ref[...]), lead[0:5, 0:6])

    @pl.when(me < half - 1)
    def _():
        send_relation(me + 1, in_outer, 0).start()

    @pl.when(me == half - 1)
    def _():
        send_relation(me + 1, in_mid, 1).start()

    @pl.when(me == half)
    def _():
        send_relation(me - 1, in_mid, 1).start()

    @pl.when(me > half)
    def _():
        send_relation(me - 1, in_outer, 0).start()

    middle = (me == half - 1) | (me == half)

    @pl.when(middle)
    def _():
        send_relation(me, in_mid, 1).wait_recv()
        gap = msg[...] - in_mid[...]
        in_x[...] = -apply(inverse(gap[:, 0:5]), gap[:, 5])

    @pl.when(jnp.logical_not(middle))
    def _():
        send_x(me).wait_recv()

    @pl.when(me < half)
    def _():
        found = apply(inv_ref[...], in_x[...] - lead[0:5, 5])

        @pl.when(me == 0)
        def _():
            lead[0:5, 6] = jnp.zeros((5,) + tile, jnp.float32)
            lead[5:10, 6] = found

        @pl.when(me > 0)
        def _():
            x_msg[...] = found
            send_x(me - 1).start()
            lead[0:5, 6] = found
            lead[5:10, 6] = apply(in_outer[:, 0:5], found) + in_outer[:, 5]

    @pl.when(me >= half)
    def _():
        x = in_x[...]
        d = apply(msg[:, 0:5], x) + msg[:, 5]
        lead[0:5, 6] = x
        lead[5:10, 6] = d

        @pl.when(me < count - 1)
        def _():
            x_msg[...] = apply(t11(), x) + apply(t12(), d) + t1()
            send_x(me + 1).start()

    z = [lead[k, 6] for k in range(10)]

    def finish(block, _):
        for u in range(rows):
            i = block * rows + u
            for r in range(5):
                terms = [basis[i, r, k] * z[k] for k in range(10)] + [basis[i, r, 10]]
                while len(terms) > 1:
                    terms = [sum(terms[k + 1:k + 2], terms[k]) for k in range(0, len(terms), 2)]
                out_ref[r, block, u, :] = terms[0].reshape(lines)
        return 0

    lax.fori_loop(0, blocks, finish, 0)

    for sends, receives, buffer, copy in halos:

        @pl.when(sends)
        def _():
            copy.wait_send()

    send_relation(me, in_outer, 0).wait_send()

    @pl.when((me > 0) & (me < count - 1))
    def _():
        send_x(me).wait_send()


def per_device(flux_x, flux_z, viscous, jacobian):
    cells, lines = viscous.shape
    rows = 8
    blocks = cells // rows
    tile = (lines // 128, 128)
    f32 = jnp.float32
    line_cells = (blocks, rows, lines)
    delta = pl.pallas_call(
        functools.partial(kernel, lax.axis_size("line"), lax.axis_size("plane")),
        out_shape=jax.ShapeDtypeStruct((5,) + line_cells, f32),
        in_specs=[pl.BlockSpec(memory_space=pl.ANY)] * 4,
        out_specs=pl.BlockSpec(memory_space=pltpu.VMEM),
        scratch_shapes=[
            pltpu.VMEM((5,) + line_cells, f32),
            pltpu.VMEM((5,) + line_cells, f32),
            pltpu.VMEM(line_cells, f32),
            pltpu.VMEM((5, 5) + line_cells, f32),
            pltpu.VMEM((5, rows, lines), f32),
            pltpu.VMEM((5, rows, lines), f32),
            pltpu.VMEM((5, blocks, rows, 128), f32),
            pltpu.VMEM((5, blocks, rows, 128), f32),
            pltpu.VMEM((5, rows, lines), f32),
            pltpu.VMEM((cells,) + tile, f32),
            pltpu.VMEM((cells, 5) + tile, f32),
            pltpu.VMEM((cells, 25) + tile, f32),
            pltpu.VMEM((cells, 5, 11) + tile, f32),
            pltpu.VMEM((10, 11) + tile, f32),
            pltpu.VMEM((5, 6) + tile, f32),
            pltpu.VMEM((5, 6) + tile, f32),
            pltpu.VMEM((5, 6) + tile, f32),
            pltpu.VMEM((5,) + tile, f32),
            pltpu.VMEM((5,) + tile, f32),
            pltpu.VMEM((5, 5) + tile, f32),
            pltpu.VMEM((5, 5) + tile, f32),
            pltpu.VMEM((10, 7) + tile, f32),
            pltpu.SemaphoreType.DMA((3,)),
            pltpu.SemaphoreType.DMA((blocks,)),
            pltpu.SemaphoreType.DMA((4,)),
            pltpu.SemaphoreType.DMA((4,)),
            pltpu.SemaphoreType.DMA((2,)),
            pltpu.SemaphoreType.DMA((3,)),
        ],
        compiler_params=pltpu.CompilerParams(
            collective_id=0, has_side_effects=True, vmem_limit_bytes=56 * 1024 * 1024
        ),
    )(
        flux_x.transpose(1, 0, 2).reshape((5,) + line_cells),
        flux_z.transpose(1, 0, 2).reshape((5,) + line_cells),
        viscous.reshape(line_cells),
        jacobian.transpose(1, 2, 0, 3).reshape((5, 5) + line_cells),
    )
    return delta.reshape(5, cells, lines).transpose(1, 0, 2)


def solution(mesh):
    placed = (
        P("line", None, "plane"),
        P("line", None, "plane"),
        P("line", "plane"),
        P("line", None, None, "plane"),
    )
    return jax.shard_map(
        per_device, mesh=mesh, in_specs=placed, out_specs=P("line", None, "plane"), check_vma=False
    )
```
